32 devices in a mesh: row: 8 (over z, x), col: 4 (over y, core).
Axes of the slice: x: 2, y: 2, z: 4, core: 2. Of those that a mesh axis runs over, the one named last changes fastest.
Arguments:
- features: float32 [4096, 128], P(('row', 'col')), may hold values from -6 to 6
- weight: float32 [128, 128], replicated, may hold values from -0.5 to 0.5
- degree: int32 [4096], P(('row', 'col')), may hold values from 1 to 64
- tiles: float32 [8, 4, 24, 128, 128], P('row', 'col'), may hold values from 0 to 6, as said below
- tile_coords: int32 [8, 4, 24, 2], P('row', 'col'), may hold values from 0 to 7, as said below
- tile_count: int32 [8, 4], P('row', 'col'), may hold values from 1 to 24, as said below
- cotangent: float32 [4096, 128], P(('row', 'col')), may hold values from -0.25 to 0.25
Outputs:
- hidden_out: float32 [4096, 128], P(('row', 'col'))
- weight_grad: float32 [128, 128], replicated
The draws below stay inside these ranges and needn't reach their ends.
Inputs may be any that keep to these rules, and one draw needn't show every extreme that they name: `tiles`: only slots below tile_count are live; the other slots hold values that are ignored. `tile_coords`: the first entry is a tile row below 4, the second a tile column below 8; within one device the pairs of all slots are distinct. `tile_count`: number of live slots of a device; the largest is reached on some device.
All inputs are finite; a program needn't handle non-finite values.
Results may differ from the reference program's by a relative error of at most 0.0003.
Values sent between devices are 32-bit elements; how exact they have to be, the bound alone decides.
A program may use at most 64 MiB of HBM per device.

```python
import jax
import jax.numpy as jnp
from jax import lax

HIDDEN_UNITS = 128
TILE_WIDTH = 128
ND = 128
TMAX = 24
RT = 4
TILE_COLUMNS = 8
NODES = 4096
N_ROW = 8
N_COL = 4


def draw_tiles(key, part):
    key = jax.random.fold_in(key, 11)
    key_mask, key_value = jax.random.split(key, 2)
    shape = (N_ROW, N_COL, TMAX, TILE_WIDTH, TILE_WIDTH)
    present = jax.random.bernoulli(key_mask, 0.5, shape).astype(jnp.float32)
    return present * jax.random.uniform(key_value, shape, jnp.float32, 0.2, 1.0)


def draw_tile_coords(key, part):
    key = jax.random.fold_in(key, 23)
    slot_total = RT * TILE_COLUMNS
    scores = jax.random.randint(key, (N_ROW, N_COL, slot_total), 0, 1 << 20) * slot_total
    scores = scores + jnp.arange(slot_total, dtype=jnp.int32)
    scores = scores.at[0, 0, slot_total - 1].set(-1)
    ranking = jnp.argsort(scores, axis=-1, stable=True)[:, :, :TMAX].astype(jnp.int32)
    return jnp.stack([ranking // TILE_COLUMNS, ranking % TILE_COLUMNS], axis=-1).astype(jnp.int32)


def draw_tile_count(key, part):
    key = jax.random.fold_in(key, 37)
    key_draw, key_pick = jax.random.split(key)
    counts = jnp.min(jax.random.randint(key_draw, (3, N_ROW, N_COL), 1, TMAX + 1), axis=0)
    position = jax.random.randint(key_pick, (), 0, N_ROW * N_COL)
    return counts.reshape(-1).at[position].set(TMAX).reshape(N_ROW, N_COL).astype(jnp.int32)


def set_ends(result, stream_key, low, largest):
    longest = result.shape.index(max(result.shape))
    spots = []
    for shift in (0, 1):
        where = [jax.random.randint(jax.random.fold_in(stream_key, axis), (), 0, length) for axis, length in enumerate(result.shape)]
        where[longest] = (where[longest] + shift) % result.shape[longest]
        spots.append(tuple(where))
    return result.at[spots[0]].set(low).at[spots[1]].set(largest)


def steps_of(stream_key, dims, pieces, low, top_value):
    loudness, own = 1.0, jax.random.fold_in(stream_key, 6)
    for dim, blocks in pieces:
        steps = jnp.exp(jax.random.uniform(jax.random.fold_in(own, dim), (blocks,), jnp.float32, low / len(pieces), top_value / len(pieces)))
        loudness = loudness * jnp.repeat(steps, dims[dim] // blocks).reshape([-1 if axis == dim else 1 for axis in range(len(dims))])
    return loudness


def gaussian(rng, dims, spread, limit, cuts=(), kind=jnp.bfloat16):
    drawn = jax.random.normal(rng, dims, jnp.float32) * spread
    if len(cuts) > 0:
        drawn = steps_of(rng, dims, cuts, -0.22, 0.18) * drawn
    return jnp.clip(drawn, min=-limit, max=limit).astype(kind)


def setup_inputs(seed: int = 0) -> dict:
    seeds = jax.random.split(jax.random.key(seed), 8)
    return {
        "features": gaussian(seeds[0], (NODES, HIDDEN_UNITS), 1.0, 6.0, ((0, 32),), jnp.float32),
        "weight": gaussian(seeds[1], (HIDDEN_UNITS, HIDDEN_UNITS), HIDDEN_UNITS ** -0.5, 0.5, (), jnp.float32),
        "degree": set_ends(jax.random.randint(seeds[2], (NODES,), 1, 65), jax.random.fold_in(seeds[2], 1), 1, 64).astype(jnp.int32),
        "tiles": draw_tiles(jax.random.fold_in(seeds[7], 71), 0),
        "tile_coords": draw_tile_coords(jax.random.fold_in(seeds[7], 71), 0),
        "tile_count": draw_tile_count(jax.random.fold_in(seeds[7], 71), 0),
        "cotangent": gaussian(seeds[6], (NODES, HIDDEN_UNITS), (NODES ** -0.5), 0.25, ((0, 32),), jnp.float32),
    }


def reference(features, weight, degree, tiles, tile_coords, tile_count, cotangent):
    exact_accumulate = lax.Precision.HIGHEST
    devices = N_ROW * N_COL
    inv_root = lax.rsqrt(degree.astype(jnp.float32))[:, None]
    projected = jnp.dot(features, weight, precision=exact_accumulate, preferred_element_type=jnp.float32) * inv_root
    col_blocks = projected.reshape(N_ROW, N_COL, ND, HIDDEN_UNITS).transpose(1, 0, 2, 3).reshape(N_COL, TILE_COLUMNS, TILE_WIDTH, HIDDEN_UNITS)
    flat_tiles = tiles.reshape(devices, TMAX, TILE_WIDTH, TILE_WIDTH)
    flat_coords = tile_coords.reshape(devices, TMAX, 2).astype(jnp.int32)
    flat_count = tile_count.reshape(devices).astype(jnp.int32)
    device_ids = jnp.arange(devices, dtype=jnp.int32)
    slot_ids = jnp.arange(TMAX, dtype=jnp.int32)
    row_ids = jnp.arange(RT, dtype=jnp.int32)
    col_ids = jnp.arange(TILE_COLUMNS, dtype=jnp.int32)

    def forward_step(totals, payload):
        tile_set, coords, live_count, device_id = payload
        block_row = device_id // N_COL
        block_col = device_id % N_COL
        live_mask = (slot_ids < live_count).astype(jnp.float32)[:, None, None]
        picked = col_blocks[block_col][coords[:, 1]]
        tile_products = jnp.einsum('tab,tbf->taf', tile_set, picked, precision=exact_accumulate) * live_mask
        indicator_matrix = (coords[:, 0][None, :] == row_ids[:, None]).astype(jnp.float32)
        value_contribution = jnp.einsum('rt,taf->raf', indicator_matrix, tile_products, precision=exact_accumulate).reshape(RT * TILE_WIDTH, HIDDEN_UNITS)
        return (totals.at[block_row].add(value_contribution), None)
    row_sums, unused = lax.scan(forward_step, jnp.zeros((N_ROW, RT * TILE_WIDTH, HIDDEN_UNITS), jnp.float32), (flat_tiles, flat_coords, flat_count, device_ids))
    aggregated = row_sums.reshape(NODES, HIDDEN_UNITS) * inv_root
    hidden_out = jax.nn.elu(aggregated)
    slope_grad = cotangent * jnp.exp(jnp.minimum(aggregated, 0.0))
    row_blocks = (slope_grad * inv_root).reshape(N_ROW, RT, TILE_WIDTH, HIDDEN_UNITS)

    def backward_step(totals, payload):
        tile_set, coords, live_count, device_id = payload
        block_row = device_id // N_COL
        block_col = device_id % N_COL
        live_mask = (slot_ids < live_count).astype(jnp.float32)[:, None, None]
        picked = row_blocks[block_row][coords[:, 0]]
        tile_products = jnp.einsum('tab,taf->tbf', tile_set, picked, precision=exact_accumulate) * live_mask
        indicator_matrix = (coords[:, 1][None, :] == col_ids[:, None]).astype(jnp.float32)
        value_contribution = jnp.einsum('vu,uam->vam', indicator_matrix, tile_products, precision=exact_accumulate).reshape(TILE_COLUMNS * TILE_WIDTH, HIDDEN_UNITS)
        return (totals.at[block_col].add(value_contribution), None)
    col_sums, unused = lax.scan(backward_step, jnp.zeros((N_COL, TILE_COLUMNS * TILE_WIDTH, HIDDEN_UNITS), jnp.float32), (flat_tiles, flat_coords, flat_count, device_ids))
    grad_proj = col_sums.reshape(N_COL, N_ROW, ND, HIDDEN_UNITS).transpose(1, 0, 2, 3).reshape(NODES, HIDDEN_UNITS) * inv_root
    weight_grad = jnp.dot(features.T, grad_proj, precision=exact_accumulate, preferred_element_type=jnp.float32)
    return (hidden_out, weight_grad)
```

```python
import functools

import jax
import jax.numpy as jnp
from jax import lax
from jax.experimental import pallas as pl
from jax.experimental.pallas import tpu as pltpu
from jax.sharding import PartitionSpec as P

F32 = jnp.float32
BF16 = jnp.bfloat16
MESH = pl.DeviceIdType.MESH


def gathered(features, weight, degree, tiles, tile_coords, tile_count, cotangent):
    exact_accumulate = lax.Precision.HIGHEST
    node_dev, feat_width = features.shape
    tile_set = tiles[0, 0]
    coords = tile_coords[0, 0]
    slot_count, tile_edge, unused_edge = tile_set.shape
    live_mask = (jnp.arange(slot_count, dtype=jnp.int32) < tile_count[0, 0]).astype(jnp.float32)[
        :, None, None
    ]
    row_tiles = lax.axis_size("col") * node_dev // tile_edge
    col_tiles = lax.axis_size("row") * node_dev // tile_edge
    row_onehot = (coords[:, 0][None, :] == jnp.arange(row_tiles, dtype=jnp.int32)[:, None]).astype(
        jnp.float32
    )
    inv_root = lax.rsqrt(degree.astype(jnp.float32))[:, None]
    outgoing = features * inv_root
    col_block = lax.all_gather(outgoing, "row", axis=0, tiled=True).reshape(
        col_tiles, tile_edge, feat_width
    )
    picked = col_block[coords[:, 1]]
    tile_products = (
        jnp.einsum("tab,tbf->taf", tile_set, picked, precision=exact_accumulate) * live_mask
    )
    row_partial = jnp.einsum("rt,taf->raf", row_onehot, tile_products, precision=exact_accumulate)
    row_partial = row_partial.reshape(row_tiles * tile_edge, feat_width)
    own_rows = lax.psum_scatter(row_partial, "col", scatter_dimension=0, tiled=True) * inv_root
    aggregated = jnp.dot(
        own_rows, weight, precision=exact_accumulate, preferred_element_type=jnp.float32
    )
    hidden_out = jax.nn.elu(aggregated)
    slope_grad = cotangent * jnp.exp(jnp.minimum(aggregated, 0.0))
    local_grad = jnp.dot(
        own_rows.T, slope_grad, precision=exact_accumulate, preferred_element_type=jnp.float32
    )
    weight_grad = lax.psum(local_grad, ("row", "col"))
    return (hidden_out, weight_grad)


def halves(v):
    hi = v.astype(BF16)
    return hi, (v - hi.astype(F32)).astype(BF16)


def dot(a, b, dims=((1,), (0,))):
    return lax.dot_general(a, b, (dims, ((), ())), preferred_element_type=F32)


def dot_split(a, b, dims=((1,), (0,))):
    a_hi, a_lo = halves(a)
    b_hi, b_lo = halves(b)
    return dot(a_hi, b_hi, dims) + dot(a_hi, b_lo, dims) + dot(a_lo, b_hi, dims)


def fused(
    n_row,
    features,
    weight,
    degree,
    tiles_hbm,
    coords,
    count,
    cotangent,
    hidden_out,
    weight_grad,
    tiles,
    nodes,
    a_hi,
    a_lo,
    acc,
    from_core,
    to_y,
    from_y,
    grad,
    terms,
    total,
    grad_all,
    codes,
    tile_sem,
    up_sem,
    down_sem,
    across_sem,
    node_sem,
    core_send,
    core_recv,
    y_send,
    y_recv,
    term_send,
    term_recv,
    all_send,
    all_recv,
):
    n_col = 4
    nz = n_row // 2
    n_dev = n_row * n_col
    slots = tiles.shape[0]
    width = features.shape[0]
    i = lax.axis_index("row")
    j = lax.axis_index("col")
    me = i * n_col + j
    z = i // 2
    x = i % 2
    y = j // 2
    core = j % 2

    def device(d):
        return {"row": d // n_col, "col": d % n_col}

    load_tiles = pltpu.make_async_copy(tiles_hbm.at[0, 0], tiles, tile_sem)
    load_tiles.start()

    barrier = pltpu.get_barrier_semaphore()

    @pl.loop(1, n_dev)
    def _(k):
        pl.semaphore_signal(
            barrier, inc=1, device_id=device((me + k) % n_dev), device_id_type=MESH
        )

    inv_row = lax.rsqrt(degree[...].astype(F32))
    eye = lax.broadcasted_iota(jnp.int32, (width, width), 0) == lax.broadcasted_iota(
        jnp.int32, (width, width), 1
    )
    inv_root = jnp.sum(
        jnp.where(eye, jnp.broadcast_to(inv_row, (width, width)), 0.0), axis=1, keepdims=True
    )
    nodes[z, pl.ds(pl.multiple_of(x * width, width), width)] = features[...] * inv_root
    pl.semaphore_wait(barrier, n_dev - 1)

    def block(zz, xx):
        return nodes.at[zz, pl.ds(pl.multiple_of(xx * width, width), width)]

    def send(zz, to_row, sem):
        return pltpu.make_async_remote_copy(
            src_ref=block(zz, x),
            dst_ref=block(zz, x),
            send_sem=sem,
            recv_sem=node_sem.at[zz, x],
            device_id={"row": to_row, "col": j},
            device_id_type=MESH,
        )

    def arrive(zz, xx):
        pltpu.make_async_copy(block(zz, xx), block(zz, xx), node_sem.at[zz, xx]).wait()

    def pass_on(zz, s, upward, downward):
        send(zz, i - x + (1 - x), across_sem.at[zz]).start()
        if upward:

            @pl.when(z + 1 < nz)
            def _():
                send(zz, i + 2, up_sem.at[s]).start()

        if downward:

            @pl.when(z > 0)
            def _():
                send(zz, i - 2, down_sem.at[s]).start()

    pass_on(z, 0, True, True)

    for t in range(slots):
        live = t < count[0, 0]
        codes[t] = jnp.where(live, coords[0, 0, t, 0] * n_row + coords[0, 0, t, 1], -1)
    load_tiles.wait()

    @pl.loop(0, nz)
    def _(zz):
        for xx in range(2):
            for r in range(n_col):
                code = r * n_row + zz * 2 + xx
                slot = jnp.int32(-1)
                for t in range(slots):
                    slot = jnp.where(codes[t] == code, jnp.int32(t), slot)
                tile = tiles[jnp.maximum(slot, 0)]
                hi, lo = halves(jnp.where(slot >= 0, tile, 0.0))
                a_hi[zz, r * width : (r + 1) * width, xx * width : (xx + 1) * width] = hi
                a_lo[zz, r * width : (r + 1) * width, xx * width : (xx + 1) * width] = lo

    acc[...] = jnp.zeros_like(acc)

    def multiply(zz):
        x_hi, x_lo = halves(nodes[zz])
        acc[...] += dot(a_hi[zz], x_hi) + dot(a_hi[zz], x_lo) + dot(a_lo[zz], x_hi)

    for s in range(nz):
        if s > 0:

            @pl.when(z - s >= 0)
            def _():
                arrive(z - s, x)
                pass_on(z - s, s, True, False)

            @pl.when(z + s < nz)
            def _():
                arrive(z + s, x)
                pass_on(z + s, s, False, True)

        if s == 0:
            arrive(z, 1 - x)
            multiply(z)
        else:

            @pl.when(z - s >= 0)
            def _():
                arrive(z - s, 1 - x)
                multiply(z - s)

            @pl.when(z + s < nz)
            def _():
                arrive(z + s, 1 - x)
                multiply(z + s)

    def part(k):
        return acc.at[pl.ds(pl.multiple_of(k * width, width), width)]

    def to_core(yy):
        return pltpu.make_async_remote_copy(
            src_ref=part(yy * 2 + 1 - core),
            dst_ref=from_core.at[yy],
            send_sem=core_send.at[yy],
            recv_sem=core_recv.at[yy],
            device_id={"row": i, "col": y * 2 + 1 - core},
            device_id_type=MESH,
        )

    far_core = to_core(1 - y)
    own_core = to_core(y)
    far_core.start()
    own_core.start()
    far_core.wait_recv()
    to_y[...] = part((1 - y) * 2 + core)[...] + from_core[1 - y]
    y_copy = pltpu.make_async_remote_copy(
        src_ref=to_y,
        dst_ref=from_y,
        send_sem=y_send,
        recv_sem=y_recv,
        device_id={"row": i, "col": (1 - y) * 2 + core},
        device_id_type=MESH,
    )
    y_copy.start()
    own_core.wait_recv()
    own_sum = part(j)[...] + from_core[y]
    y_copy.wait_recv()
    own_rows = (own_sum + from_y[...]) * inv_root
    aggregated = dot_split(own_rows, weight[...])
    grown = jnp.exp(jnp.minimum(aggregated, 0.0))
    slope = cotangent[...] * grown
    local_grad = dot_split(own_rows, slope, ((0,), (0,)))
    rows = width // n_dev
    grad[...] = local_grad.reshape(n_dev, rows, width)

    @pl.loop(1, n_dev)
    def _(k):
        d = (me + k) % n_dev
        pltpu.make_async_remote_copy(
            src_ref=grad.at[d],
            dst_ref=terms.at[n_dev - 1 - k],
            send_sem=term_send,
            recv_sem=term_recv,
            device_id=device(d),
            device_id_type=MESH,
        ).start()

    hidden_out[...] = jnp.where(aggregated > 0.0, aggregated, grown - 1.0)
    pltpu.make_async_copy(terms, terms, term_recv).wait()
    total[...] = grad[me] + jnp.sum(terms[...], axis=0)

    @pl.loop(1, n_dev)
    def _(k):
        d = (me + k) % n_dev
        pltpu.make_async_remote_copy(
            src_ref=total,
            dst_ref=grad_all.at[me],
            send_sem=all_send,
            recv_sem=all_recv,
            device_id=device(d),
            device_id_type=MESH,
        ).start()

    pltpu.make_async_copy(terms, terms, all_recv).wait()
    grad_all[me] = total[...]
    weight_grad[...] = grad_all[...].reshape(width, width)

    pltpu.make_async_copy(terms, terms, term_send).wait()
    pltpu.make_async_copy(terms, terms, all_send).wait()
    send(z, i, across_sem.at[z]).wait_send()
    far_core.wait_send()
    own_core.wait_send()
    y_copy.wait_send()

    def sent(sem):
        pltpu.make_async_copy(block(0, 0), block(0, 0), sem).wait()

    for s in range(nz):
        if s > 0:

            @pl.when(z - s >= 0)
            def _():
                sent(across_sem.at[z - s])

            @pl.when(z + s < nz)
            def _():
                sent(across_sem.at[z + s])

        @pl.when((z - s >= 0) & (z + 1 < nz))
        def _():
            sent(up_sem.at[s])

        @pl.when((z + s < nz) & (z > 0))
        def _():
            sent(down_sem.at[s])


def dense(features, weight, degree, tiles, tile_coords, tile_count, cotangent):
    n_row = lax.axis_size("row")
    n_col = lax.axis_size("col")
    n_dev = n_row * n_col
    nz = n_row // 2
    width, feat = features.shape
    slots = tiles.shape[2]
    rows = width // n_dev
    vmem = pl.BlockSpec(memory_space=pltpu.VMEM)
    smem = pl.BlockSpec(memory_space=pltpu.SMEM)
    dma = pltpu.SemaphoreType.DMA
    return pl.pallas_call(
        functools.partial(fused, n_row),
        out_shape=(
            jax.ShapeDtypeStruct((width, feat), F32),
            jax.ShapeDtypeStruct((feat, feat), F32),
        ),
        in_specs=[vmem, vmem, vmem, pl.BlockSpec(memory_space=pl.ANY), smem, smem, vmem],
        out_specs=(vmem, vmem),
        scratch_shapes=[
            pltpu.VMEM((slots, width, width), F32),
            pltpu.VMEM((nz, 2 * width, feat), F32),
            pltpu.VMEM((nz, n_col * width, 2 * width), BF16),
            pltpu.VMEM((nz, n_col * width, 2 * width), BF16),
            pltpu.VMEM((n_col * width, feat), F32),
            pltpu.VMEM((2, width, feat), F32),
            pltpu.VMEM((width, feat), F32),
            pltpu.VMEM((width, feat), F32),
            pltpu.VMEM((n_dev, rows, feat), F32),
            pltpu.VMEM((n_dev - 1, rows, feat), F32),
            pltpu.VMEM((rows, feat), F32),
            pltpu.VMEM((n_dev, rows, feat), F32),
            pltpu.SMEM((slots,), jnp.int32),
            dma,
            dma((nz,)),
            dma((nz,)),
            dma((nz,)),
            dma((nz, 2)),
            dma((2,)),
            dma((2,)),
            dma,
            dma,
            dma,
            dma,
            dma,
            dma,
        ],
        compiler_params=pltpu.CompilerParams(
            collective_id=0, has_side_effects=True, vmem_limit_bytes=32 * 1024 * 1024
        ),
    )(features, weight, degree.reshape(1, width), tiles, tile_coords, tile_count, cotangent)


def solution(mesh):
    n_row, n_col = mesh.shape["row"], mesh.shape["col"]

    def local(features, weight, degree, tiles, tile_coords, tile_count, cotangent):
        width, feat = features.shape
        small = n_row * n_col <= 2 * tiles.shape[2] and n_row % 2 == 0 and n_col == 4
        small = small and tiles.shape[3] == width and width % (n_row * n_col) == 0
        form = dense if small and feat == width else gathered
        return form(features, weight, degree, tiles, tile_coords, tile_count, cotangent)

    return jax.shard_map(
        local,
        mesh=mesh,
        in_specs=(
            P(("row", "col"), None),
            P(),
            P(("row", "col")),
            P("row", "col", None, None, None),
            P("row", "col", None, None),
            P("row", "col"),
            P(("row", "col"), None),
        ),
        out_specs=(P(("row", "col"), None), P()),
        check_vma=False,
    )
```

```python
import functools

import jax
import jax.numpy as jnp
from jax import lax
from jax.experimental import pallas as pl
from jax.experimental.pallas import tpu as pltpu
from jax.sharding import PartitionSpec as P

F32 = jnp.float32
BF16 = jnp.bfloat16
MESH = pl.DeviceIdType.MESH


def gathered(features, weight, degree, tiles, tile_coords, tile_count, cotangent):
    exact_accumulate = lax.Precision.HIGHEST
    node_dev, feat_width = features.shape
    tile_set = tiles[0, 0]
    coords = tile_coords[0, 0]
    slot_count, tile_edge, unused_edge = tile_set.shape
    live_mask = (jnp.arange(slot_count, dtype=jnp.int32) < tile_count[0, 0]).astype(jnp.float32)[
        :, None, None
    ]
    row_tiles = lax.axis_size("col") * node_dev // tile_edge
    col_tiles = lax.axis_size("row") * node_dev // tile_edge
    row_onehot = (coords[:, 0][None, :] == jnp.arange(row_tiles, dtype=jnp.int32)[:, None]).astype(
        jnp.float32
    )
    inv_root = lax.rsqrt(degree.astype(jnp.float32))[:, None]
    outgoing = features * inv_root
    col_block = lax.all_gather(outgoing, "row", axis=0, tiled=True).reshape(
        col_tiles, tile_edge, feat_width
    )
    picked = col_block[coords[:, 1]]
    tile_products = (
        jnp.einsum("tab,tbf->taf", tile_set, picked, precision=exact_accumulate) * live_mask
    )
    row_partial = jnp.einsum("rt,taf->raf", row_onehot, tile_products, precision=exact_accumulate)
    row_partial = row_partial.reshape(row_tiles * tile_edge, feat_width)
    own_rows = lax.psum_scatter(row_partial, "col", scatter_dimension=0, tiled=True) * inv_root
    aggregated = jnp.dot(
        own_rows, weight, precision=exact_accumulate, preferred_element_type=jnp.float32
    )
    hidden_out = jax.nn.elu(aggregated)
    slope_grad = cotangent * jnp.exp(jnp.minimum(aggregated, 0.0))
    local_grad = jnp.dot(
        own_rows.T, slope_grad, precision=exact_accumulate, preferred_element_type=jnp.float32
    )
    weight_grad = lax.psum(local_grad, ("row", "col"))
    return (hidden_out, weight_grad)


def halves(v):
    hi = v.astype(BF16)
    return hi, (v - hi.astype(F32)).astype(BF16)


def dot(a, b, dims=((1,), (0,))):
    return lax.dot_general(a, b, (dims, ((), ())), preferred_element_type=F32)


def dot_split(a, b, dims=((1,), (0,))):
    a_hi, a_lo = halves(a)
    b_hi, b_lo = halves(b)
    return dot(a_hi, b_hi, dims) + dot(a_hi, b_lo, dims) + dot(a_lo, b_hi, dims)


def fused(
    n_row,
    features_hbm,
    weight_hbm,
    degree_hbm,
    tiles_hbm,
    coords,
    count,
    cotangent_hbm,
    hidden_out,
    weight_grad,
    features,
    weight,
    degree,
    cotangent,
    tiles,
    nodes,
    a_hi,
    a_lo,
    acc,
    from_core,
    to_y,
    from_y,
    grad,
    terms,
    layers,
    codes,
    load_sem,
    line_sem,
    across_sem,
    node_sem,
    core_send,
    core_recv,
    y_send,
    y_recv,
    term_send,
    term_recv,
    layer_send,
    layer_recv,
    all_send,
    all_recv,
):
    n_col = 4
    nz = n_row // 2
    slots = tiles.shape[0]
    width = features.shape[0]
    i = lax.axis_index("row")
    j = lax.axis_index("col")
    me = i * n_col + j
    z = i // 2
    x = i % 2
    y = j // 2
    core = j % 2

    loads = [
        pltpu.make_async_copy(source, target, load_sem.at[k])
        for k, (source, target) in enumerate(
            (
                (degree_hbm, degree),
                (features_hbm, features),
                (tiles_hbm.at[0, 0], tiles),
                (weight_hbm, weight),
                (cotangent_hbm, cotangent),
            )
        )
    ]
    for load in loads:
        load.start()

    barrier = pltpu.get_barrier_semaphore()

    friends = [{"row": (i + 2 * s) % n_row, "col": j} for s in range(1, nz)]
    friends.append({"row": z * 2 + 1 - x, "col": j})
    friends.append({"row": i, "col": y * 2 + 1 - core})
    friends.append({"row": i, "col": (1 - y) * 2 + core})
    for friend in friends:
        pl.semaphore_signal(barrier, inc=1, device_id=friend, device_id_type=MESH)

    loads[0].wait()
    inv_row = lax.rsqrt(degree[...].astype(F32))
    eye = lax.broadcasted_iota(jnp.int32, (width, width), 0) == lax.broadcasted_iota(
        jnp.int32, (width, width), 1
    )
    inv_root = jnp.sum(
        jnp.where(eye, jnp.broadcast_to(inv_row, (width, width)), 0.0), axis=1, keepdims=True
    )
    loads[1].wait()
    nodes[z, pl.ds(pl.multiple_of(x * width, width), width)] = features[...] * inv_root
    pl.semaphore_wait(barrier, len(friends))

    step = width // 2

    def block(zz, xx, h):
        return nodes.at[zz, pl.ds(pl.multiple_of(xx * width + h * step, step), step)]

    def send(zz, h, to_row, sem):
        return pltpu.make_async_remote_copy(
            src_ref=block(zz, x, h),
            dst_ref=block(zz, x, h),
            send_sem=sem,
            recv_sem=node_sem.at[zz, x, h],
            device_id={"row": to_row, "col": j},
            device_id_type=MESH,
        )

    def arrive(zz, xx, h):
        pltpu.make_async_copy(block(zz, xx, h), block(zz, xx, h), node_sem.at[zz, xx, h]).wait()

    def at_distance(s, act):
        @pl.when(z + s < nz)
        def _():
            act(z + s)

        @pl.when(z - s >= 0)
        def _():
            act(z - s)

    def across(zz, h):
        send(zz, h, z * 2 + 1 - x, across_sem.at[zz, h]).start()

    for h in range(2):
        across(z, h)
    for s in range(nz - 1, 0, -1):
        for h in range(2):
            at_distance(s, lambda t, h=h: send(z, h, t * 2 + x, line_sem.at[t, h]).start())

    for t in range(slots):
        live = t < count[0, 0]
        codes[t] = jnp.where(live, coords[0, t] * n_row + coords[1, t], -1)
    loads[2].wait()
    loads[3].wait()
    loads[4].wait()

    @pl.loop(0, nz)
    def _(zz):
        for xx in range(2):
            for r in range(n_col):
                code = r * n_row + zz * 2 + xx
                slot = jnp.int32(-1)
                for t in range(slots):
                    slot = jnp.where(codes[t] == code, jnp.int32(t), slot)
                tile = tiles[jnp.maximum(slot, 0)]
                hi, lo = halves(jnp.where(slot >= 0, tile, 0.0))
                a_hi[zz, r * width : (r + 1) * width, xx * width : (xx + 1) * width] = hi
                a_lo[zz, r * width : (r + 1) * width, xx * width : (xx + 1) * width] = lo

    acc[...] = jnp.zeros_like(acc)

    def multiply(zz):
        x_hi, x_lo = halves(nodes[zz])
        acc[...] += dot(a_hi[zz], x_hi) + dot(a_hi[zz], x_lo) + dot(a_lo[zz], x_hi)

    def pass_on(zz, h):
        arrive(zz, x, h)
        across(zz, h)

    def finish(zz):
        arrive(zz, 1 - x, 0)
        arrive(zz, 1 - x, 1)
        multiply(zz)

    for s in range(1, nz):
        for h in range(2):
            at_distance(s, lambda t, h=h: pass_on(t, h))
    finish(z)
    for s in range(1, nz):
        at_distance(s, finish)

    def part(k):
        return acc.at[pl.ds(pl.multiple_of(k * width, width), width)]

    def to_core(yy):
        return pltpu.make_async_remote_copy(
            src_ref=part(yy * 2 + 1 - core),
            dst_ref=from_core.at[yy],
            send_sem=core_send.at[yy],
            recv_sem=core_recv.at[yy],
            device_id={"row": i, "col": y * 2 + 1 - core},
            device_id_type=MESH,
        )

    far_core = to_core(1 - y)
    own_core = to_core(y)
    far_core.start()
    own_core.start()
    far_core.wait_recv()
    to_y[...] = part((1 - y) * 2 + core)[...] + from_core[1 - y]
    y_copy = pltpu.make_async_remote_copy(
        src_ref=to_y,
        dst_ref=from_y,
        send_sem=y_send,
        recv_sem=y_recv,
        device_id={"row": i, "col": (1 - y) * 2 + core},
        device_id_type=MESH,
    )
    y_copy.start()
    own_core.wait_recv()
    own_sum = part(j)[...] + from_core[y]
    y_copy.wait_recv()
    own_rows = (own_sum + from_y[...]) * inv_root
    aggregated = dot_split(own_rows, weight[...])
    grown = jnp.exp(jnp.minimum(aggregated, 0.0))
    slope = cotangent[...] * grown
    local_grad = dot_split(own_rows, slope, ((0,), (0,)))
    grad[...] = local_grad
    n_plane = 2 * n_col
    rows = width // n_plane
    mine = x * n_col + j

    def piece(k):
        return pl.ds(pl.multiple_of(k * rows, rows), rows)

    def member(k):
        return {"row": z * 2 + k // n_col, "col": k % n_col}

    for k in range(1, n_plane):
        other = (mine + k) % n_plane
        pltpu.make_async_remote_copy(
            src_ref=grad.at[piece(other)],
            dst_ref=terms.at[n_plane - 1 - k],
            send_sem=term_send,
            recv_sem=term_recv,
            device_id=member(other),
            device_id_type=MESH,
        ).start()

    hidden_out[...] = jnp.where(aggregated > 0.0, aggregated, grown - 1.0)
    pltpu.make_async_copy(terms, terms, term_recv).wait()
    layers[z] = grad[piece(mine)] + jnp.sum(terms[...], axis=0)
    for s in range(1, nz):
        pltpu.make_async_remote_copy(
            src_ref=layers.at[z],
            dst_ref=layers.at[z],
            send_sem=layer_send,
            recv_sem=layer_recv,
            device_id={"row": (i + 2 * s) % n_row, "col": j},
            device_id_type=MESH,
        ).start()
    others = layers.at[pl.ds(0, nz - 1)]
    pltpu.make_async_copy(others, others, layer_recv).wait()
    weight_grad[piece(mine)] = jnp.sum(layers[...], axis=0)
    for k in range(1, n_plane):
        pltpu.make_async_remote_copy(
            src_ref=weight_grad.at[piece(mine)],
            dst_ref=weight_grad.at[piece(mine)],
            send_sem=all_send,
            recv_sem=all_recv,
            device_id=member((mine + k) % n_plane),
            device_id_type=MESH,
        ).start()

    pltpu.make_async_copy(terms, terms, all_recv).wait()

    pltpu.make_async_copy(terms, terms, term_send).wait()
    pltpu.make_async_copy(others, others, layer_send).wait()
    pltpu.make_async_copy(terms, terms, all_send).wait()
    far_core.wait_send()
    own_core.wait_send()
    y_copy.wait_send()

    def sent(sem, h):
        pltpu.make_async_copy(block(0, 0, h), block(0, 0, h), sem).wait()

    for h in range(2):
        sent(across_sem.at[z, h], h)
        for s in range(1, nz):
            at_distance(s, lambda t, h=h: sent(across_sem.at[t, h], h))
            at_distance(s, lambda t, h=h: sent(line_sem.at[t, h], h))


def dense(features, weight, degree, tiles, tile_coords, tile_count, cotangent):
    n_row = lax.axis_size("row")
    n_col = lax.axis_size("col")
    nz = n_row // 2
    width, feat = features.shape
    slots = tiles.shape[2]
    rows = width // (2 * n_col)
    vmem = pl.BlockSpec(memory_space=pltpu.VMEM)
    hbm = pl.BlockSpec(memory_space=pltpu.HBM)
    smem = pl.BlockSpec(memory_space=pltpu.SMEM)
    dma = pltpu.SemaphoreType.DMA
    return pl.pallas_call(
        functools.partial(fused, n_row),
        out_shape=(
            jax.ShapeDtypeStruct((width, feat), F32),
            jax.ShapeDtypeStruct((feat, feat), F32),
        ),
        in_specs=[hbm, hbm, hbm, hbm, smem, smem, hbm],
        out_specs=(vmem, vmem),
        scratch_shapes=[
            pltpu.VMEM((width, feat), F32),
            pltpu.VMEM((feat, feat), F32),
            pltpu.VMEM((1, width), jnp.int32),
            pltpu.VMEM((width, feat), F32),
            pltpu.VMEM((slots, width, width), F32),
            pltpu.VMEM((nz, 2 * width, feat), F32),
            pltpu.VMEM((nz, n_col * width, 2 * width), BF16),
            pltpu.VMEM((nz, n_col * width, 2 * width), BF16),
            pltpu.VMEM((n_col * width, feat), F32),
            pltpu.VMEM((2, width, feat), F32),
            pltpu.VMEM((width, feat), F32),
            pltpu.VMEM((width, feat), F32),
            pltpu.VMEM((width, feat), F32),
            pltpu.VMEM((2 * n_col - 1, rows, feat), F32),
            pltpu.VMEM((nz, rows, feat), F32),
            pltpu.SMEM((slots,), jnp.int32),
            dma((5,)),
            dma((nz, 2)),
            dma((nz, 2)),
            dma((nz, 2, 2)),
            dma((2,)),
            dma((2,)),
            dma,
            dma,
            dma,
            dma,
            dma,
            dma,
            dma,
            dma,
        ],
        compiler_params=pltpu.CompilerParams(
            collective_id=0, has_side_effects=True, vmem_limit_bytes=62 * 1024 * 1024
        ),
    )(
        features,
        weight,
        degree.reshape(1, width),
        tiles,
        tile_coords[0, 0].T,
        tile_count,
        cotangent,
    )


def solution(mesh):
    n_row, n_col = mesh.shape["row"], mesh.shape["col"]

    def local(features, weight, degree, tiles, tile_coords, tile_count, cotangent):
        width, feat = features.shape
        small = n_row * n_col <= 2 * tiles.shape[2] and n_row % 2 == 0 and n_col == 4
        small = small and tiles.shape[3] == width and width % (32 * n_col) == 0
        form = dense if small and feat == width else gathered
        return form(features, weight, degree, tiles, tile_coords, tile_count, cotangent)

    return jax.shard_map(
        local,
        mesh=mesh,
        in_specs=(
            P(("row", "col"), None),
            P(),
            P(("row", "col")),
            P("row", "col", None, None, None),
            P("row", "col", None, None),
            P("row", "col"),
            P(("row", "col"), None),
        ),
        out_specs=(P(("row", "col"), None), P()),
        check_vma=False,
    )
```

```python
import functools

import jax
import jax.numpy as jnp
from jax import lax
from jax.experimental import pallas as pl
from jax.experimental.pallas import tpu as pltpu
from jax.sharding import PartitionSpec as P

F32 = jnp.float32
BF16 = jnp.bfloat16
MESH = pl.DeviceIdType.MESH


def gathered(features, weight, degree, tiles, tile_coords, tile_count, cotangent):
    exact_accumulate = lax.Precision.HIGHEST
    node_dev, feat_width = features.shape
    tile_set = tiles[0, 0]
    coords = tile_coords[0, 0]
    slot_count, tile_edge, unused_edge = tile_set.shape
    live_mask = (jnp.arange(slot_count, dtype=jnp.int32) < tile_count[0, 0]).astype(jnp.float32)[
        :, None, None
    ]
    row_tiles = lax.axis_size("col") * node_dev // tile_edge
    col_tiles = lax.axis_size("row") * node_dev // tile_edge
    row_onehot = (coords[:, 0][None, :] == jnp.arange(row_tiles, dtype=jnp.int32)[:, None]).astype(
        jnp.float32
    )
    inv_root = lax.rsqrt(degree.astype(jnp.float32))[:, None]
    outgoing = features * inv_root
    col_block = lax.all_gather(outgoing, "row", axis=0, tiled=True).reshape(
        col_tiles, tile_edge, feat_width
    )
    picked = col_block[coords[:, 1]]
    tile_products = (
        jnp.einsum("tab,tbf->taf", tile_set, picked, precision=exact_accumulate) * live_mask
    )
    row_partial = jnp.einsum("rt,taf->raf", row_onehot, tile_products, precision=exact_accumulate)
    row_partial = row_partial.reshape(row_tiles * tile_edge, feat_width)
    own_rows = lax.psum_scatter(row_partial, "col", scatter_dimension=0, tiled=True) * inv_root
    aggregated = jnp.dot(
        own_rows, weight, precision=exact_accumulate, preferred_element_type=jnp.float32
    )
    hidden_out = jax.nn.elu(aggregated)
    slope_grad = cotangent * jnp.exp(jnp.minimum(aggregated, 0.0))
    local_grad = jnp.dot(
        own_rows.T, slope_grad, precision=exact_accumulate, preferred_element_type=jnp.float32
    )
    weight_grad = lax.psum(local_grad, ("row", "col"))
    return (hidden_out, weight_grad)


def halves(v):
    hi = v.astype(BF16)
    return hi, (v - hi.astype(F32)).astype(BF16)


def dot(a, b, dims=((1,), (0,))):
    return lax.dot_general(a, b, (dims, ((), ())), preferred_element_type=F32)


def dot_split(a, b, dims=((1,), (0,))):
    a_hi, a_lo = halves(a)
    b_hi, b_lo = halves(b)
    return dot(a_hi, b_hi, dims) + dot(a_hi, b_lo, dims) + dot(a_lo, b_hi, dims)


def fused(
    n_row,
    features_hbm,
    weight_hbm,
    degree_hbm,
    tiles_hbm,
    coords,
    count,
    cotangent_hbm,
    hidden_out,
    weight_grad,
    features,
    weight,
    degree,
    cotangent,
    tiles,
    nodes,
    a_hi,
    a_lo,
    acc,
    from_core,
    to_y,
    from_y,
    grad,
    terms,
    layers,
    codes,
    load_sem,
    line_sem,
    across_sem,
    node_sem,
    core_send,
    core_recv,
    y_send,
    y_recv,
    term_send,
    term_recv,
    layer_send,
    layer_recv,
    all_send,
    all_recv,
):
    n_col = 4
    nz = n_row // 2
    slots = tiles.shape[0]
    width = features.shape[0]
    i = lax.axis_index("row")
    j = lax.axis_index("col")
    me = i * n_col + j
    z = i // 2
    x = i % 2
    y = j // 2
    core = j % 2

    loads = [
        pltpu.make_async_copy(source, target, load_sem.at[k])
        for k, (source, target) in enumerate(
            (
                (degree_hbm, degree),
                (features_hbm, features),
                (tiles_hbm.at[0, 0], tiles),
                (weight_hbm, weight),
                (cotangent_hbm, cotangent),
            )
        )
    ]
    for load in loads:
        load.start()

    barrier = pltpu.get_barrier_semaphore()

    friends = [{"row": (i + 2 * s) % n_row, "col": j} for s in range(1, nz)]
    friends.append({"row": z * 2 + 1 - x, "col": j})
    friends.append({"row": i, "col": y * 2 + 1 - core})
    friends.append({"row": i, "col": (1 - y) * 2 + core})
    for friend in friends:
        pl.semaphore_signal(barrier, inc=1, device_id=friend, device_id_type=MESH)

    loads[0].wait()
    inv_row = lax.rsqrt(degree[...].astype(F32))
    eye = lax.broadcasted_iota(jnp.int32, (width, width), 0) == lax.broadcasted_iota(
        jnp.int32, (width, width), 1
    )
    inv_root = jnp.sum(
        jnp.where(eye, jnp.broadcast_to(inv_row, (width, width)), 0.0), axis=1, keepdims=True
    )
    loads[1].wait()
    nodes[z, pl.ds(pl.multiple_of(x * width, width), width)] = features[...] * inv_root
    pl.semaphore_wait(barrier, len(friends))

    step = width // 2

    def block(zz, xx, h):
        return nodes.at[zz, pl.ds(pl.multiple_of(xx * width + h * step, step), step)]

    def send(zz, h, to_row, sem):
        return pltpu.make_async_remote_copy(
            src_ref=block(zz, x, h),
            dst_ref=block(zz, x, h),
            send_sem=sem,
            recv_sem=node_sem.at[zz, x, h],
            device_id={"row": to_row, "col": j},
            device_id_type=MESH,
        )

    def arrive(zz, xx, h):
        pltpu.make_async_copy(block(zz, xx, h), block(zz, xx, h), node_sem.at[zz, xx, h]).wait()

    def at_distance(s, act):
        @pl.when(z + s < nz)
        def _():
            act(z + s)

        @pl.when(z - s >= 0)
        def _():
            act(z - s)

    def across(zz, h):
        send(zz, h, z * 2 + 1 - x, across_sem.at[zz, h]).start()

    for h in range(2):
        across(z, h)
    for s in range(nz - 1, 0, -1):
        for h in range(2):
            at_distance(s, lambda t, h=h: send(z, h, t * 2 + x, line_sem.at[t, h]).start())

    for t in range(slots):
        live = t < count[0, 0]
        codes[t] = jnp.where(live, coords[0, t] * n_row + coords[1, t], -1)
    loads[2].wait()
    loads[3].wait()
    loads[4].wait()

    @pl.loop(0, nz)
    def _(zz):
        for xx in range(2):
            for r in range(n_col):
                code = r * n_row + zz * 2 + xx
                slot = jnp.int32(-1)
                for t in range(slots):
                    slot = jnp.where(codes[t] == code, jnp.int32(t), slot)
                tile = tiles[jnp.maximum(slot, 0)]
                hi, lo = halves(jnp.where(slot >= 0, tile, 0.0))
                a_hi[zz, r * width : (r + 1) * width, xx * width : (xx + 1) * width] = hi
                a_lo[zz, r * width : (r + 1) * width, xx * width : (xx + 1) * width] = lo

    acc[...] = jnp.zeros_like(acc)

    def multiply(zz):
        x_hi, x_lo = halves(nodes[zz])
        acc[...] += dot(a_hi[zz], x_hi) + dot(a_hi[zz], x_lo) + dot(a_lo[zz], x_hi)

    def pass_on(zz, h):
        arrive(zz, x, h)
        across(zz, h)

    def finish(zz):
        arrive(zz, 1 - x, 0)
        arrive(zz, 1 - x, 1)
        multiply(zz)

    for s in range(1, nz):
        for h in range(2):
            at_distance(s, lambda t, h=h: pass_on(t, h))
    finish(z)
    for s in range(1, nz):
        at_distance(s, finish)

    def part(k):
        return acc.at[pl.ds(pl.multiple_of(k * width, width), width)]

    def to_core(yy):
        return pltpu.make_async_remote_copy(
            src_ref=part(yy * 2 + 1 - core),
            dst_ref=from_core.at[yy],
            send_sem=core_send.at[yy],
            recv_sem=core_recv.at[yy],
            device_id={"row": i, "col": y * 2 + 1 - core},
            device_id_type=MESH,
        )

    far_core = to_core(1 - y)
    own_core = to_core(y)
    far_core.start()
    own_core.start()
    far_core.wait_recv()
    to_y[...] = part((1 - y) * 2 + core)[...] + from_core[1 - y]
    y_copy = pltpu.make_async_remote_copy(
        src_ref=to_y,
        dst_ref=from_y,
        send_sem=y_send,
        recv_sem=y_recv,
        device_id={"row": i, "col": (1 - y) * 2 + core},
        device_id_type=MESH,
    )
    y_copy.start()
    own_core.wait_recv()
    own_sum = part(j)[...] + from_core[y]
    y_copy.wait_recv()
    own_rows = (own_sum + from_y[...]) * inv_root
    aggregated = dot_split(own_rows, weight[...])
    grown = jnp.exp(jnp.minimum(aggregated, 0.0))
    slope = cotangent[...] * grown
    local_grad = dot_split(own_rows, slope, ((0,), (0,)))
    grad[...] = local_grad
    n_plane = 2 * n_col
    rows = width // n_plane
    mine = x * n_col + j

    def piece(k):
        return pl.ds(pl.multiple_of(k * rows, rows), rows)

    def member(k):
        return {"row": z * 2 + k // n_col, "col": k % n_col}

    for k in range(1, n_plane):
        other = (mine + k) % n_plane
        pltpu.make_async_remote_copy(
            src_ref=grad.at[piece(other)],
            dst_ref=terms.at[n_plane - 1 - k],
            send_sem=term_send,
            recv_sem=term_recv,
            device_id=member(other),
            device_id_type=MESH,
        ).start()

    hidden_out[...] = jnp.where(aggregated > 0.0, aggregated, grown - 1.0)
    pltpu.make_async_copy(terms, terms, term_recv).wait()
    layers[z] = grad[piece(mine)] + jnp.sum(terms[...], axis=0)
    for s in range(1, nz):
        pltpu.make_async_remote_copy(
            src_ref=layers.at[z],
            dst_ref=layers.at[z],
            send_sem=layer_send,
            recv_sem=layer_recv,
            device_id={"row": (i + 2 * s) % n_row, "col": j},
            device_id_type=MESH,
        ).start()
    others = layers.at[pl.ds(0, nz - 1)]
    pltpu.make_async_copy(others, others, layer_recv).wait()
    weight_grad[piece(mine)] = jnp.sum(layers[...], axis=0)
    for k in range(1, n_plane):
        pltpu.make_async_remote_copy(
            src_ref=weight_grad.at[piece(mine)],
            dst_ref=weight_grad.at[piece(mine)],
            send_sem=all_send,
            recv_sem=all_recv,
            device_id=member((mine + k) % n_plane),
            device_id_type=MESH,
        ).start()

    pltpu.make_async_copy(terms, terms, all_recv).wait()

    pltpu.make_async_copy(terms, terms, term_send).wait()
    pltpu.make_async_copy(others, others, layer_send).wait()
    pltpu.make_async_copy(terms, terms, all_send).wait()
    far_core.wait_send()
    own_core.wait_send()
    y_copy.wait_send()

    def sent(sem, h):
        pltpu.make_async_copy(block(0, 0, h), block(0, 0, h), sem).wait()

    for h in range(2):
        sent(across_sem.at[z, h], h)
        for s in range(1, nz):
            at_distance(s, lambda t, h=h: sent(across_sem.at[t, h], h))
            at_distance(s, lambda t, h=h: sent(line_sem.at[t, h], h))


def dense(features, weight, degree, tiles, tile_coords, tile_count, cotangent):
    n_row = lax.axis_size("row")
    n_col = lax.axis_size("col")
    nz = n_row // 2
    width, feat = features.shape
    slots = tiles.shape[2]
    rows = width // (2 * n_col)
    vmem = pl.BlockSpec(memory_space=pltpu.VMEM)
    hbm = pl.BlockSpec(memory_space=pltpu.HBM)
    smem = pl.BlockSpec(memory_space=pltpu.SMEM)
    dma = pltpu.SemaphoreType.DMA
    return pl.pallas_call(
        functools.partial(fused, n_row),
        out_shape=(pltpu.VMEM((width, feat), F32), pltpu.VMEM((feat, feat), F32)),
        in_specs=[hbm, hbm, hbm, hbm, smem, smem, hbm],
        out_specs=(vmem, vmem),
        scratch_shapes=[
            pltpu.VMEM((width, feat), F32),
            pltpu.VMEM((feat, feat), F32),
            pltpu.VMEM((1, width), jnp.int32),
            pltpu.VMEM((width, feat), F32),
            pltpu.VMEM((slots, width, width), F32),
            pltpu.VMEM((nz, 2 * width, feat), F32),
            pltpu.VMEM((nz, n_col * width, 2 * width), BF16),
            pltpu.VMEM((nz, n_col * width, 2 * width), BF16),
            pltpu.VMEM((n_col * width, feat), F32),
            pltpu.VMEM((2, width, feat), F32),
            pltpu.VMEM((width, feat), F32),
            pltpu.VMEM((width, feat), F32),
            pltpu.VMEM((width, feat), F32),
            pltpu.VMEM((2 * n_col - 1, rows, feat), F32),
            pltpu.VMEM((nz, rows, feat), F32),
            pltpu.SMEM((slots,), jnp.int32),
            dma((5,)),
            dma((nz, 2)),
            dma((nz, 2)),
            dma((nz, 2, 2)),
            dma((2,)),
            dma((2,)),
            dma,
            dma,
            dma,
            dma,
            dma,
            dma,
            dma,
            dma,
        ],
        compiler_params=pltpu.CompilerParams(
            collective_id=0, has_side_effects=True, vmem_limit_bytes=56 * 1024 * 1024
        ),
    )(
        features,
        weight,
        degree.reshape(1, width),
        tiles,
        tile_coords[0, 0].T,
        tile_count,
        cotangent,
    )


def solution(mesh):
    n_row, n_col = mesh.shape["row"], mesh.shape["col"]

    def local(features, weight, degree, tiles, tile_coords, tile_count, cotangent):
        width, feat = features.shape
        small = n_row * n_col <= 2 * tiles.shape[2] and n_row % 2 == 0 and n_col == 4
        small = small and tiles.shape[3] == width and width % (32 * n_col) == 0
        form = dense if small and feat == width else gathered
        return form(features, weight, degree, tiles, tile_coords, tile_count, cotangent)

    return jax.shard_map(
        local,
        mesh=mesh,
        in_specs=(
            P(("row", "col"), None),
            P(),
            P(("row", "col")),
            P("row", "col", None, None, None),
            P("row", "col", None, None),
            P("row", "col"),
            P(("row", "col"), None),
        ),
        out_specs=(P(("row", "col"), None), P()),
        check_vma=False,
    )
```

```python
import functools

import jax
import jax.numpy as jnp
from jax import lax
from jax.experimental import pallas as pl
from jax.experimental.pallas import tpu as pltpu
from jax.sharding import PartitionSpec as P

F32 = jnp.float32
BF16 = jnp.bfloat16
MESH = pl.DeviceIdType.MESH


def gathered(features, weight, degree, tiles, tile_coords, tile_count, cotangent):
    exact_accumulate = lax.Precision.HIGHEST
    node_dev, feat_width = features.shape
    tile_set = tiles[0, 0]
    coords = tile_coords[0, 0]
    slot_count, tile_edge, unused_edge = tile_set.shape
    live_mask = (jnp.arange(slot_count, dtype=jnp.int32) < tile_count[0, 0]).astype(jnp.float32)[
        :, None, None
    ]
    row_tiles = lax.axis_size("col") * node_dev // tile_edge
    col_tiles = lax.axis_size("row") * node_dev // tile_edge
    row_onehot = (coords[:, 0][None, :] == jnp.arange(row_tiles, dtype=jnp.int32)[:, None]).astype(
        jnp.float32
    )
    inv_root = lax.rsqrt(degree.astype(jnp.float32))[:, None]
    outgoing = features * inv_root
    col_block = lax.all_gather(outgoing, "row", axis=0, tiled=True).reshape(
        col_tiles, tile_edge, feat_width
    )
    picked = col_block[coords[:, 1]]
    tile_products = (
        jnp.einsum("tab,tbf->taf", tile_set, picked, precision=exact_accumulate) * live_mask
    )
    row_partial = jnp.einsum("rt,taf->raf", row_onehot, tile_products, precision=exact_accumulate)
    row_partial = row_partial.reshape(row_tiles * tile_edge, feat_width)
    own_rows = lax.psum_scatter(row_partial, "col", scatter_dimension=0, tiled=True) * inv_root
    aggregated = jnp.dot(
        own_rows, weight, precision=exact_accumulate, preferred_element_type=jnp.float32
    )
    hidden_out = jax.nn.elu(aggregated)
    slope_grad = cotangent * jnp.exp(jnp.minimum(aggregated, 0.0))
    local_grad = jnp.dot(
        own_rows.T, slope_grad, precision=exact_accumulate, preferred_element_type=jnp.float32
    )
    weight_grad = lax.psum(local_grad, ("row", "col"))
    return (hidden_out, weight_grad)


def halves(v):
    hi = v.astype(BF16)
    return hi, (v - hi.astype(F32)).astype(BF16)


def dot(a, b, dims=((1,), (0,))):
    return lax.dot_general(a, b, (dims, ((), ())), preferred_element_type=F32)


def dot_split(a, b, dims=((1,), (0,))):
    a_hi, a_lo = halves(a)
    b_hi, b_lo = halves(b)
    return dot(a_hi, b_hi, dims) + dot(a_hi, b_lo, dims) + dot(a_lo, b_hi, dims)


def fused(
    n_row,
    features_hbm,
    weight_hbm,
    degree_hbm,
    tiles_hbm,
    coords,
    count,
    cotangent_hbm,
    hidden_out,
    weight_grad,
    features,
    weight,
    degree,
    cotangent,
    tiles,
    nodes,
    a_hi,
    a_lo,
    acc,
    from_core,
    to_y,
    from_y,
    grad,
    terms,
    layers,
    codes,
    load_sem,
    send_sem,
    node_sem,
    core_send,
    core_recv,
    y_send,
    y_recv,
    term_send,
    term_recv,
    layer_send,
    layer_recv,
    all_send,
    all_recv,
):
    n_col = 4
    nz = n_row // 2
    slots = tiles.shape[0]
    width = features.shape[0]
    i = lax.axis_index("row")
    j = lax.axis_index("col")
    me = i * n_col + j
    z = i // 2
    x = i % 2
    y = j // 2
    core = j % 2

    loads = [
        pltpu.make_async_copy(source, target, load_sem.at[k])
        for k, (source, target) in enumerate(
            (
                (degree_hbm, degree),
                (features_hbm, features),
                (tiles_hbm.at[0, 0], tiles),
                (weight_hbm, weight),
                (cotangent_hbm, cotangent),
            )
        )
    ]
    for load in loads:
        load.start()

    barrier = pltpu.get_barrier_semaphore()

    friends = [{"row": (i + 2 * s) % n_row, "col": j} for s in range(1, nz)]
    friends.append({"row": z * 2 + 1 - x, "col": j})
    friends.append({"row": i, "col": y * 2 + 1 - core})
    friends.append({"row": i, "col": (1 - y) * 2 + core})
    for friend in friends:
        pl.semaphore_signal(barrier, inc=1, device_id=friend, device_id_type=MESH)

    loads[0].wait()
    inv_row = lax.rsqrt(degree[...].astype(F32))
    eye = lax.broadcasted_iota(jnp.int32, (width, width), 0) == lax.broadcasted_iota(
        jnp.int32, (width, width), 1
    )
    inv_root = jnp.sum(
        jnp.where(eye, jnp.broadcast_to(inv_row, (width, width)), 0.0), axis=1, keepdims=True
    )
    loads[1].wait()
    nodes[z, pl.ds(pl.multiple_of(x * width, width), width)] = features[...] * inv_root
    pl.semaphore_wait(barrier, len(friends))

    step = width // 2

    def block(zz, xx, h):
        return nodes.at[zz, pl.ds(pl.multiple_of(xx * width + h * step, step), step)]

    def send(zz, h, to_row, sem):
        return pltpu.make_async_remote_copy(
            src_ref=block(zz, x, h),
            dst_ref=block(zz, x, h),
            send_sem=sem,
            recv_sem=node_sem.at[zz, x, h],
            device_id={"row": to_row, "col": j},
            device_id_type=MESH,
        )

    def arrive(zz, xx, h):
        pltpu.make_async_copy(block(zz, xx, h), block(zz, xx, h), node_sem.at[zz, xx, h]).wait()

    def at_distance(s, act):
        @pl.when(z + s < nz)
        def _():
            act(z + s)

        @pl.when(z - s >= 0)
        def _():
            act(z - s)

    def across(zz, h):
        send(zz, h, z * 2 + 1 - x, send_sem).start()

    for h in range(2):
        across(z, h)
    for s in range(nz - 1, 0, -1):
        for h in range(2):
            at_distance(s, lambda t, h=h: send(z, h, t * 2 + x, send_sem).start())

    for t in range(slots):
        live = t < count[0, 0]
        codes[t] = jnp.where(live, coords[0, t] * n_row + coords[1, t], -1)
    loads[2].wait()
    loads[3].wait()
    loads[4].wait()

    @pl.loop(0, nz)
    def _(zz):
        for xx in range(2):
            for r in range(n_col):
                code = r * n_row + zz * 2 + xx
                slot = jnp.int32(-1)
                for t in range(slots):
                    slot = jnp.where(codes[t] == code, jnp.int32(t), slot)
                tile = tiles[jnp.maximum(slot, 0)]
                hi, lo = halves(jnp.where(slot >= 0, tile, 0.0))
                a_hi[zz, r * width : (r + 1) * width, xx * width : (xx + 1) * width] = hi
                a_lo[zz, r * width : (r + 1) * width, xx * width : (xx + 1) * width] = lo

    acc[...] = jnp.zeros_like(acc)

    def multiply(zz):
        x_hi, x_lo = halves(nodes[zz])
        acc[...] += dot(a_hi[zz], x_hi) + dot(a_hi[zz], x_lo) + dot(a_lo[zz], x_hi)

    def pass_on(zz, h):
        arrive(zz, x, h)
        across(zz, h)

    def finish(zz):
        arrive(zz, 1 - x, 0)
        arrive(zz, 1 - x, 1)
        multiply(zz)

    for s in range(1, nz):
        for h in range(2):
            at_distance(s, lambda t, h=h: pass_on(t, h))
    finish(z)
    for s in range(1, nz):
        at_distance(s, finish)

    def part(k):
        return acc.at[pl.ds(pl.multiple_of(k * width, width), width)]

    def to_core(yy):
        return pltpu.make_async_remote_copy(
            src_ref=part(yy * 2 + 1 - core),
            dst_ref=from_core.at[yy],
            send_sem=core_send.at[yy],
            recv_sem=core_recv.at[yy],
            device_id={"row": i, "col": y * 2 + 1 - core},
            device_id_type=MESH,
        )

    far_core = to_core(1 - y)
    own_core = to_core(y)
    far_core.start()
    own_core.start()
    far_core.wait_recv()
    to_y[...] = part((1 - y) * 2 + core)[...] + from_core[1 - y]
    y_copy = pltpu.make_async_remote_copy(
        src_ref=to_y,
        dst_ref=from_y,
        send_sem=y_send,
        recv_sem=y_recv,
        device_id={"row": i, "col": (1 - y) * 2 + core},
        device_id_type=MESH,
    )
    y_copy.start()
    own_core.wait_recv()
    own_sum = part(j)[...] + from_core[y]
    y_copy.wait_recv()
    own_rows = (own_sum + from_y[...]) * inv_root
    aggregated = dot_split(own_rows, weight[...])
    grown = jnp.exp(jnp.minimum(aggregated, 0.0))
    slope = cotangent[...] * grown
    local_grad = dot_split(own_rows, slope, ((0,), (0,)))
    grad[...] = local_grad
    n_plane = 2 * n_col
    rows = width // n_plane
    mine = x * n_col + j

    def piece(k):
        return pl.ds(pl.multiple_of(k * rows, rows), rows)

    def member(k):
        return {"row": z * 2 + k // n_col, "col": k % n_col}

    for k in range(1, n_plane):
        other = (mine + k) % n_plane
        pltpu.make_async_remote_copy(
            src_ref=grad.at[piece(other)],
            dst_ref=terms.at[n_plane - 1 - k],
            send_sem=term_send,
            recv_sem=term_recv,
            device_id=member(other),
            device_id_type=MESH,
        ).start()

    hidden_out[...] = jnp.where(aggregated > 0.0, aggregated, grown - 1.0)
    pltpu.make_async_copy(terms, terms, term_recv).wait()
    layers[z] = grad[piece(mine)] + jnp.sum(terms[...], axis=0)
    for s in range(1, nz):
        pltpu.make_async_remote_copy(
            src_ref=layers.at[z],
            dst_ref=layers.at[z],
            send_sem=layer_send,
            recv_sem=layer_recv,
            device_id={"row": (i + 2 * s) % n_row, "col": j},
            device_id_type=MESH,
        ).start()
    others = layers.at[pl.ds(0, nz - 1)]
    pltpu.make_async_copy(others, others, layer_recv).wait()
    weight_grad[piece(mine)] = jnp.sum(layers[...], axis=0)
    for k in range(1, n_plane):
        pltpu.make_async_remote_copy(
            src_ref=weight_grad.at[piece(mine)],
            dst_ref=weight_grad.at[piece(mine)],
            send_sem=all_send,
            recv_sem=all_recv,
            device_id=member((mine + k) % n_plane),
            device_id_type=MESH,
        ).start()

    pltpu.make_async_copy(terms, terms, all_recv).wait()

    pltpu.make_async_copy(terms, terms, term_send).wait()
    pltpu.make_async_copy(others, others, layer_send).wait()
    pltpu.make_async_copy(terms, terms, all_send).wait()
    far_core.wait_send()
    own_core.wait_send()
    y_copy.wait_send()

    sent = tiles.at[pl.ds(0, n_row - 1)]
    pltpu.make_async_copy(sent, sent, send_sem).wait()


def dense(features, weight, degree, tiles, tile_coords, tile_count, cotangent):
    n_row = lax.axis_size("row")
    n_col = lax.axis_size("col")
    nz = n_row // 2
    width, feat = features.shape
    slots = tiles.shape[2]
    rows = width // (2 * n_col)
    vmem = pl.BlockSpec(memory_space=pltpu.VMEM)
    hbm = pl.BlockSpec(memory_space=pltpu.HBM)
    smem = pl.BlockSpec(memory_space=pltpu.SMEM)
    dma = pltpu.SemaphoreType.DMA
    return pl.pallas_call(
        functools.partial(fused, n_row),
        out_shape=(pltpu.VMEM((width, feat), F32), pltpu.VMEM((feat, feat), F32)),
        in_specs=[hbm, hbm, hbm, hbm, smem, smem, hbm],
        out_specs=(vmem, vmem),
        scratch_shapes=[
            pltpu.VMEM((width, feat), F32),
            pltpu.VMEM((feat, feat), F32),
            pltpu.VMEM((1, width), jnp.int32),
            pltpu.VMEM((width, feat), F32),
            pltpu.VMEM((slots, width, width), F32),
            pltpu.VMEM((nz, 2 * width, feat), F32),
            pltpu.VMEM((nz, n_col * width, 2 * width), BF16),
            pltpu.VMEM((nz, n_col * width, 2 * width), BF16),
            pltpu.VMEM((n_col * width, feat), F32),
            pltpu.VMEM((2, width, feat), F32),
            pltpu.VMEM((width, feat), F32),
            pltpu.VMEM((width, feat), F32),
            pltpu.VMEM((width, feat), F32),
            pltpu.VMEM((2 * n_col - 1, rows, feat), F32),
            pltpu.VMEM((nz, rows, feat), F32),
            pltpu.SMEM((slots,), jnp.int32),
            dma((5,)),
            dma,
            dma((nz, 2, 2)),
            dma((2,)),
            dma((2,)),
            dma,
            dma,
            dma,
            dma,
            dma,
            dma,
            dma,
            dma,
        ],
        compiler_params=pltpu.CompilerParams(
            collective_id=0, has_side_effects=True, vmem_limit_bytes=56 * 1024 * 1024
        ),
    )(
        features,
        weight,
        degree.reshape(1, width),
        tiles,
        tile_coords[0, 0].T,
        tile_count,
        cotangent,
    )


def solution(mesh):
    n_row, n_col = mesh.shape["row"], mesh.shape["col"]

    def local(features, weight, degree, tiles, tile_coords, tile_count, cotangent):
        width, feat = features.shape
        small = n_row * n_col <= 2 * tiles.shape[2] and n_row % 2 == 0 and n_col == 4
        small = small and tiles.shape[3] == width and width % (32 * n_col) == 0 and n_row <= tiles.shape[2]
        form = dense if small and feat == width else gathered
        return form(features, weight, degree, tiles, tile_coords, tile_count, cotangent)

    return jax.shard_map(
        local,
        mesh=mesh,
        in_specs=(
            P(("row", "col"), None),
            P(),
            P(("row", "col")),
            P("row", "col", None, None, None),
            P("row", "col", None, None),
            P("row", "col"),
            P(("row", "col"), None),
        ),
        out_specs=(P(("row", "col"), None), P()),
        check_vma=False,
    )
```

```python
import functools

import jax
import jax.numpy as jnp
from jax import lax
from jax.experimental import pallas as pl
from jax.experimental.pallas import tpu as pltpu
from jax.sharding import PartitionSpec as P

F32 = jnp.float32
BF16 = jnp.bfloat16
MESH = pl.DeviceIdType.MESH


def gathered(features, weight, degree, tiles, tile_coords, tile_count, cotangent):
    exact_accumulate = lax.Precision.HIGHEST
    node_dev, feat_width = features.shape
    tile_set = tiles[0, 0]
    coords = tile_coords[0, 0]
    slot_count, tile_edge, unused_edge = tile_set.shape
    live_mask = (jnp.arange(slot_count, dtype=jnp.int32) < tile_count[0, 0]).astype(jnp.float32)[
        :, None, None
    ]
    row_tiles = lax.axis_size("col") * node_dev // tile_edge
    col_tiles = lax.axis_size("row") * node_dev // tile_edge
    row_onehot = (coords[:, 0][None, :] == jnp.arange(row_tiles, dtype=jnp.int32)[:, None]).astype(
        jnp.float32
    )
    inv_root = lax.rsqrt(degree.astype(jnp.float32))[:, None]
    outgoing = features * inv_root
    col_block = lax.all_gather(outgoing, "row", axis=0, tiled=True).reshape(
        col_tiles, tile_edge, feat_width
    )
    picked = col_block[coords[:, 1]]
    tile_products = (
        jnp.einsum("tab,tbf->taf", tile_set, picked, precision=exact_accumulate) * live_mask
    )
    row_partial = jnp.einsum("rt,taf->raf", row_onehot, tile_products, precision=exact_accumulate)
    row_partial = row_partial.reshape(row_tiles * tile_edge, feat_width)
    own_rows = lax.psum_scatter(row_partial, "col", scatter_dimension=0, tiled=True) * inv_root
    aggregated = jnp.dot(
        own_rows, weight, precision=exact_accumulate, preferred_element_type=jnp.float32
    )
    hidden_out = jax.nn.elu(aggregated)
    slope_grad = cotangent * jnp.exp(jnp.minimum(aggregated, 0.0))
    local_grad = jnp.dot(
        own_rows.T, slope_grad, precision=exact_accumulate, preferred_element_type=jnp.float32
    )
    weight_grad = lax.psum(local_grad, ("row", "col"))
    return (hidden_out, weight_grad)


def halves(v):
    hi = v.astype(BF16)
    return hi, (v - hi.astype(F32)).astype(BF16)


def dot(a, b, dims=((1,), (0,))):
    return lax.dot_general(a, b, (dims, ((), ())), preferred_element_type=F32)


def dot_split(a, b, dims=((1,), (0,))):
    a_hi, a_lo = halves(a)
    b_hi, b_lo = halves(b)
    return dot(a_hi, b_hi, dims) + dot(a_hi, b_lo, dims) + dot(a_lo, b_hi, dims)


def fused(
    n_row,
    features_hbm,
    weight_hbm,
    degree_hbm,
    tiles_hbm,
    coords,
    count,
    cotangent_hbm,
    hidden_out,
    weight_grad,
    features,
    weight,
    degree,
    cotangent,
    tiles,
    nodes,
    a_hi,
    a_lo,
    acc,
    from_core,
    to_y,
    from_y,
    grad,
    terms,
    layers,
    codes,
    load_sem,
    send_sem,
    node_sem,
    core_send,
    core_recv,
    y_send,
    y_recv,
    term_send,
    term_recv,
    layer_send,
    layer_recv,
    all_send,
    all_recv,
):
    n_col = 4
    nz = n_row // 2
    slots = tiles.shape[0]
    width = features.shape[0]
    i = lax.axis_index("row")
    j = lax.axis_index("col")
    me = i * n_col + j
    z = i // 2
    x = i % 2
    y = j // 2
    core = j % 2

    loads = [
        pltpu.make_async_copy(source, target, load_sem.at[k])
        for k, (source, target) in enumerate(
            (
                (degree_hbm, degree),
                (features_hbm, features),
                (tiles_hbm.at[0, 0], tiles),
                (weight_hbm, weight),
                (cotangent_hbm, cotangent),
            )
        )
    ]
    for load in loads:
        load.start()

    barrier = pltpu.get_barrier_semaphore()

    friends = [{"row": (i + 2 * s) % n_row, "col": j} for s in range(1, nz)]
    friends.append({"row": z * 2 + 1 - x, "col": j})
    friends.append({"row": i, "col": y * 2 + 1 - core})
    friends.append({"row": i, "col": (1 - y) * 2 + core})
    for friend in friends:
        pl.semaphore_signal(barrier, inc=1, device_id=friend, device_id_type=MESH)

    loads[0].wait()
    inv_row = lax.rsqrt(degree[...].astype(F32))
    eye = lax.broadcasted_iota(jnp.int32, (width, width), 0) == lax.broadcasted_iota(
        jnp.int32, (width, width), 1
    )
    inv_root = jnp.sum(
        jnp.where(eye, jnp.broadcast_to(inv_row, (width, width)), 0.0), axis=1, keepdims=True
    )
    loads[1].wait()
    nodes[z, pl.ds(pl.multiple_of(x * width, width), width)] = features[...] * inv_root
    pl.semaphore_wait(barrier, len(friends))

    step = width // 4

    def block(zz, xx, h):
        return nodes.at[zz, pl.ds(pl.multiple_of(xx * width + h * step, step), step)]

    def send(zz, h, to_row, sem):
        return pltpu.make_async_remote_copy(
            src_ref=block(zz, x, h),
            dst_ref=block(zz, x, h),
            send_sem=sem,
            recv_sem=node_sem.at[zz, x, h],
            device_id={"row": to_row, "col": j},
            device_id_type=MESH,
        )

    def arrive(zz, xx, h):
        pltpu.make_async_copy(block(zz, xx, h), block(zz, xx, h), node_sem.at[zz, xx, h]).wait()

    def at_distance(s, act):
        @pl.when(z + s < nz)
        def _():
            act(z + s)

        @pl.when(z - s >= 0)
        def _():
            act(z - s)

    def across(zz, h):
        send(zz, h, z * 2 + 1 - x, send_sem).start()

    for h in range(4):
        across(z, h)
    for s in range(nz - 1, 0, -1):
        for h in range(4):
            at_distance(s, lambda t, h=h: send(z, h, t * 2 + x, send_sem).start())

    for t in range(slots):
        live = t < count[0, 0]
        codes[t] = jnp.where(live, coords[0, t] * n_row + coords[1, t], -1)
    loads[2].wait()
    loads[3].wait()
    loads[4].wait()

    @pl.loop(0, nz)
    def _(zz):
        for xx in range(2):
            for r in range(n_col):
                code = r * n_row + zz * 2 + xx
                slot = jnp.int32(-1)
                for t in range(slots):
                    slot = jnp.where(codes[t] == code, jnp.int32(t), slot)
                tile = tiles[jnp.maximum(slot, 0)]
                hi, lo = halves(jnp.where(slot >= 0, tile, 0.0))
                a_hi[zz, r * width : (r + 1) * width, xx * width : (xx + 1) * width] = hi
                a_lo[zz, r * width : (r + 1) * width, xx * width : (xx + 1) * width] = lo

    acc[...] = jnp.zeros_like(acc)

    def multiply(zz):
        x_hi, x_lo = halves(nodes[zz])
        acc[...] += dot(a_hi[zz], x_hi) + dot(a_hi[zz], x_lo) + dot(a_lo[zz], x_hi)

    def pass_on(zz, h):
        arrive(zz, x, h)
        across(zz, h)

    def finish(zz):
        for h in range(4):
            arrive(zz, 1 - x, h)
        multiply(zz)

    for s in range(1, nz):
        for h in range(4):
            at_distance(s, lambda t, h=h: pass_on(t, h))
    finish(z)
    for s in range(1, nz):
        at_distance(s, finish)

    def part(k):
        return acc.at[pl.ds(pl.multiple_of(k * width, width), width)]

    def to_core(yy):
        return pltpu.make_async_remote_copy(
            src_ref=part(yy * 2 + 1 - core),
            dst_ref=from_core.at[yy],
            send_sem=core_send.at[yy],
            recv_sem=core_recv.at[yy],
            device_id={"row": i, "col": y * 2 + 1 - core},
            device_id_type=MESH,
        )

    far_core = to_core(1 - y)
    own_core = to_core(y)
    far_core.start()
    own_core.start()
    far_core.wait_recv()
    to_y[...] = part((1 - y) * 2 + core)[...] + from_core[1 - y]
    y_copy = pltpu.make_async_remote_copy(
        src_ref=to_y,
        dst_ref=from_y,
        send_sem=y_send,
        recv_sem=y_recv,
        device_id={"row": i, "col": (1 - y) * 2 + core},
        device_id_type=MESH,
    )
    y_copy.start()
    own_core.wait_recv()
    own_sum = part(j)[...] + from_core[y]
    y_copy.wait_recv()
    own_rows = (own_sum + from_y[...]) * inv_root
    aggregated = dot_split(own_rows, weight[...])
    grown = jnp.exp(jnp.minimum(aggregated, 0.0))
    slope = cotangent[...] * grown
    local_grad = dot_split(own_rows, slope, ((0,), (0,)))
    grad[...] = local_grad
    n_plane = 2 * n_col
    rows = width // n_plane
    mine = x * n_col + j

    def piece(k):
        return pl.ds(pl.multiple_of(k * rows, rows), rows)

    def member(k):
        return {"row": z * 2 + k // n_col, "col": k % n_col}

    for k in range(1, n_plane):
        other = (mine + k) % n_plane
        pltpu.make_async_remote_copy(
            src_ref=grad.at[piece(other)],
            dst_ref=terms.at[n_plane - 1 - k],
            send_sem=term_send,
            recv_sem=term_recv,
            device_id=member(other),
            device_id_type=MESH,
        ).start()

    hidden_out[...] = jnp.where(aggregated > 0.0, aggregated, grown - 1.0)
    pltpu.make_async_copy(terms, terms, term_recv).wait()
    layers[z] = grad[piece(mine)] + jnp.sum(terms[...], axis=0)
    for s in range(1, nz):
        pltpu.make_async_remote_copy(
            src_ref=layers.at[z],
            dst_ref=layers.at[z],
            send_sem=layer_send,
            recv_sem=layer_recv,
            device_id={"row": (i + 2 * s) % n_row, "col": j},
            device_id_type=MESH,
        ).start()
    others = layers.at[pl.ds(0, nz - 1)]
    pltpu.make_async_copy(others, others, layer_recv).wait()
    weight_grad[piece(mine)] = jnp.sum(layers[...], axis=0)
    for k in range(1, n_plane):
        pltpu.make_async_remote_copy(
            src_ref=weight_grad.at[piece(mine)],
            dst_ref=weight_grad.at[piece(mine)],
            send_sem=all_send,
            recv_sem=all_recv,
            device_id=member((mine + k) % n_plane),
            device_id_type=MESH,
        ).start()

    pltpu.make_async_copy(terms, terms, all_recv).wait()

    pltpu.make_async_copy(terms, terms, term_send).wait()
    pltpu.make_async_copy(others, others, layer_send).wait()
    pltpu.make_async_copy(terms, terms, all_send).wait()
    far_core.wait_send()
    own_core.wait_send()
    y_copy.wait_send()

    sent = tiles.at[pl.ds(0, n_row - 1)]
    pltpu.make_async_copy(sent, sent, send_sem).wait()


def dense(features, weight, degree, tiles, tile_coords, tile_count, cotangent):
    n_row = lax.axis_size("row")
    n_col = lax.axis_size("col")
    nz = n_row // 2
    width, feat = features.shape
    slots = tiles.shape[2]
    rows = width // (2 * n_col)
    vmem = pl.BlockSpec(memory_space=pltpu.VMEM)
    hbm = pl.BlockSpec(memory_space=pltpu.HBM)
    smem = pl.BlockSpec(memory_space=pltpu.SMEM)
    dma = pltpu.SemaphoreType.DMA
    return pl.pallas_call(
        functools.partial(fused, n_row),
        out_shape=(pltpu.VMEM((width, feat), F32), pltpu.VMEM((feat, feat), F32)),
        in_specs=[hbm, hbm, hbm, hbm, smem, smem, hbm],
        out_specs=(vmem, vmem),
        scratch_shapes=[
            pltpu.VMEM((width, feat), F32),
            pltpu.VMEM((feat, feat), F32),
            pltpu.VMEM((1, width), jnp.int32),
            pltpu.VMEM((width, feat), F32),
            pltpu.VMEM((slots, width, width), F32),
            pltpu.VMEM((nz, 2 * width, feat), F32),
            pltpu.VMEM((nz, n_col * width, 2 * width), BF16),
            pltpu.VMEM((nz, n_col * width, 2 * width), BF16),
            pltpu.VMEM((n_col * width, feat), F32),
            pltpu.VMEM((2, width, feat), F32),
            pltpu.VMEM((width, feat), F32),
            pltpu.VMEM((width, feat), F32),
            pltpu.VMEM((width, feat), F32),
            pltpu.VMEM((2 * n_col - 1, rows, feat), F32),
            pltpu.VMEM((nz, rows, feat), F32),
            pltpu.SMEM((slots,), jnp.int32),
            dma((5,)),
            dma,
            dma((nz, 2, 4)),
            dma((2,)),
            dma((2,)),
            dma,
            dma,
            dma,
            dma,
            dma,
            dma,
            dma,
            dma,
        ],
        compiler_params=pltpu.CompilerParams(
            collective_id=0, has_side_effects=True, vmem_limit_bytes=56 * 1024 * 1024
        ),
    )(
        features,
        weight,
        degree.reshape(1, width),
        tiles,
        tile_coords[0, 0].T,
        tile_count,
        cotangent,
    )


def solution(mesh):
    n_row, n_col = mesh.shape["row"], mesh.shape["col"]

    def local(features, weight, degree, tiles, tile_coords, tile_count, cotangent):
        width, feat = features.shape
        small = n_row * n_col <= 2 * tiles.shape[2] and n_row % 2 == 0 and n_col == 4
        small = small and tiles.shape[3] == width and width % (32 * n_col) == 0 and n_row <= tiles.shape[2]
        form = dense if small and feat == width else gathered
        return form(features, weight, degree, tiles, tile_coords, tile_count, cotangent)

    return jax.shard_map(
        local,
        mesh=mesh,
        in_specs=(
            P(("row", "col"), None),
            P(),
            P(("row", "col")),
            P("row", "col", None, None, None),
            P("row", "col", None, None),
            P("row", "col"),
            P(("row", "col"), None),
        ),
        out_specs=(P(("row", "col"), None), P()),
        check_vma=False,
    )
```
